512 devices in a mesh: band: 8 (over y, x_lo), space: 64 (over z, x_hi, core).
Axes of the slice: x: 4 (x_hi: 2, x_lo: 2; x = x_hi * 2 + x_lo), y: 4, z: 16, core: 2. Of those that a mesh axis runs over, the one named last changes fastest.
Arguments:
- orbitals: bfloat16 [256, 512, 16, 128], P('band', 'space'), may hold values from -6 to 6
- filters: float32 [3, 14], replicated, may hold values from -1.5 to 1.5
- panels: bfloat16 [256, 256], P('band'), may hold values from -0.375 to 0.375
Outputs:
- rotated: bfloat16 [256, 512, 16, 128], P('band', 'space')
- kinetic_rows: float32 [256, 256], P('band')
The draws below stay inside these ranges and needn't reach their ends.
All inputs are finite; a program needn't handle non-finite values.
Results may differ from the reference program's by a relative error of at most 0.0049.
Values may be sent and summed in bfloat16 or wider, within the bound.
A program may use at most 64 MiB of HBM per device.

```python
import jax
import jax.numpy as jnp
from jax import lax

NY = 16
NZ = 128
TAPS = 14
NORB = 256
NX = 512


def levels(stream_key, extent, shards, smallest, largest):
    def one(axis_at, blocks):
        steps = jax.random.uniform(jax.random.fold_in(jax.random.fold_in(stream_key, 6), axis_at), (blocks,), jnp.float32, smallest / len(shards), largest / len(shards))
        return jnp.repeat(jnp.exp(steps), extent[axis_at] // blocks).reshape((-1,) + (1,) * (len(extent) - axis_at - 1))

    gain = one(*shards[0])
    for cut in shards[1:]:
        gain = gain * one(*cut)
    return gain


def gaussian(stream_key, dims, width, reach, pieces=(), dtype=jnp.bfloat16):
    values = jax.random.normal(stream_key, dims, jnp.float32) * width
    if len(pieces) > 0:
        values = levels(stream_key, dims, pieces, -0.22, 0.18) * values
    return jnp.clip(values, min=-reach, max=reach).astype(dtype)


def setup_inputs(seed: int = 0) -> dict:
    keys = jax.random.split(jax.random.key(seed), 4)
    orbitals = gaussian(keys[0], (NORB, NX, NY, NZ), 1.0, 6.0, ((0, 8), (1, 64)))
    filters = gaussian(keys[1], (3, TAPS), TAPS ** -0.5, 1.5, (), jnp.float32)
    panels = gaussian(keys[2], (NORB, NORB), NORB ** -0.5, 0.375, ((0, 8),))
    return dict(orbitals=orbitals, filters=filters, panels=panels)


def one_pass(field, taps, axis):
    count = field.shape[axis]
    widths = [(0, 0)] * field.ndim
    widths[axis] = (7, 6)
    padded = jnp.pad(field, widths)
    total = jnp.zeros(field.shape, jnp.float32)
    for k in range(14):
        total = total + taps[k] * lax.slice_in_dim(padded, k, k + count, axis=axis)
    return total


def kinetic_one(field, filters):
    values = field.astype(jnp.float32)
    total = one_pass(values, filters[0], 0) + one_pass(values, filters[1], 1) + one_pass(values, filters[2], 2)
    return total.astype(jnp.bfloat16)


def reference(orbitals, filters, panels):
    image = lax.map(lambda field: kinetic_one(field, filters), orbitals)
    flat_img = image.reshape(NORB, -1)
    flat_psi = orbitals.reshape(NORB, -1)
    rotated = jnp.dot(panels, flat_img, preferred_element_type=jnp.float32).astype(jnp.bfloat16)
    kinetic = lax.dot_general(flat_psi, flat_img, (((1,), (1,)), ((), ())), preferred_element_type=jnp.float32)
    kinetic = kinetic * (1.0 / (NX * NY * NZ))
    return rotated.reshape(orbitals.shape), kinetic
```

```python
import functools

import jax
import jax.numpy as jnp
from jax import lax
from jax.experimental import pallas as pl
from jax.experimental.pallas import tpu as pltpu
from jax.sharding import PartitionSpec as P

MESH = pl.DeviceIdType.MESH
F32, BF16 = jnp.float32, jnp.bfloat16
BEFORE, AFTER = 7, 6
NY, NX = 4, 2
NG = 4
ORB, PLANES, ROWS, LANES = 32, 8, 16, 128
CHUNKS = PLANES // NY
ALL = ORB * NY * NX


def band_matrix(taps, row):
    a = lax.broadcasted_iota(jnp.int32, (LANES, LANES), 0)
    b = lax.broadcasted_iota(jnp.int32, (LANES, LANES), 1)
    total = jnp.zeros((LANES, LANES), F32)
    for k in range(14):
        total = jnp.where(a - b == k - BEFORE, taps[row, k], total)
    high = total.astype(BF16)
    low = (total - high.astype(F32)).astype(BF16)
    return jnp.concatenate([high, low], axis=0)


def kernel(
    nz,
    taps, psi, panels,
    out, kin,
    left, right, acc, img, psi_all, img_all, rot, own_panels, kacc, ky, kg, kz, kzs, zmat,
    halo_send, halo_recv, psi_send, psi_recv, pan_send, pan_recv, img_send, img_recv,
    fwd_send, fwd_recv, rot_send, rot_recv, ky_send, ky_recv, kg_send, kg_recv, kz_send, kz_recv, ka_send, ka_recv,
):
    band, space = lax.axis_index("band"), lax.axis_index("space")
    y, xl = band // NX, band % NX
    z, g = space // NG, space % NG
    slabs = nz * NG

    def y_peer(k):
        return lax.rem(y + k, NY)

    def remote(src, dst, send, recv, b, s):
        return pltpu.make_async_remote_copy(
            src_ref=src, dst_ref=dst, send_sem=send, recv_sem=recv, device_id=(b, s), device_id_type=MESH
        )

    partner = y * NX + (1 - xl)

    barrier = pltpu.get_barrier_semaphore()

    def greet(b, s):
        pl.semaphore_signal(barrier, inc=1, device_id=(b, s), device_id_type=MESH)

    for k in range(1, NY):
        greet(y_peer(k) * NX + xl, space)
    greet(partner, space)
    greet(band, lax.rem(space + 1, slabs))
    greet(band, lax.rem(space + slabs - 1, slabs))
    for k in range(1, NG):
        greet(band, z * NG + lax.rem(g + k, NG))

    def greet_z(k, carry):
        greet(band, lax.rem(z + k, nz) * NG + g)
        return carry

    lax.fori_loop(1, nz, greet_z, 0)
    pl.semaphore_wait(barrier, NY - 1 + 1 + 2 + NG - 1 + nz - 1)

    up = remote(psi.at[pl.ds(PLANES - BEFORE, BEFORE)], left, halo_send.at[0], halo_recv.at[0], band, space + 1)
    split = 2
    down = [
        remote(psi.at[pl.ds(0, split)], right.at[pl.ds(0, split)], halo_send.at[1], halo_recv.at[1], band, space - 1),
        remote(
            psi.at[pl.ds(split, AFTER - split)], right.at[pl.ds(split, AFTER - split)],
            halo_send.at[2], halo_recv.at[2], band, space - 1,
        ),
    ]
    first, last = space == 0, space == slabs - 1

    @pl.when(jnp.logical_not(last))
    def _():
        up.start()

    @pl.when(jnp.logical_not(first))
    def _():
        down[0].start()
        down[1].start()

    def psi_copy(k, c):
        to = y_peer(k)
        return remote(
            psi.at[c * NY + to], psi_all.at[c, :, pl.ds(pl.multiple_of(y * ORB, ORB), ORB), :],
            psi_send.at[k, c], psi_recv.at[k, c], to * NX + xl, space,
        )

    def panel_copy(k):
        return remote(
            panels, own_panels.at[pl.ds(pl.multiple_of(y * ORB, ORB), ORB), :],
            pan_send.at[k], pan_recv.at[k], y_peer(k) * NX + xl, space,
        )

    for k in (1, 3, 2):
        panel_copy(k).start()
        for c in range(CHUNKS):
            psi_copy(k, c).start()
    mine = pl.ds(pl.multiple_of(y * ORB, ORB), ORB)
    own_panels[mine, :] = panels[...]
    for c in range(CHUNKS):
        psi_all[c, :, mine, :] = psi[c * NY + y]

    @pl.when(first)
    def _():
        left[...] = jnp.zeros(left.shape, BF16)

    @pl.when(last)
    def _():
        right[...] = jnp.zeros(right.shape, BF16)

    zmat[...] = band_matrix(taps, 2)

    def along_z(p, carry):
        v = psi[p].reshape(ROWS * ORB, LANES)
        r = jnp.dot(jnp.concatenate([v, v], axis=1), zmat[...], preferred_element_type=F32)
        acc[p] = r.reshape(ROWS, ORB, LANES)
        return carry

    lax.fori_loop(0, PLANES, along_z, 0)

    half = 16

    def along_y(i, carry):
        p, h = i // 2, pl.ds(pl.multiple_of((i % 2) * half, half), half)
        v = [psi[p, r, h, :].astype(F32) for r in range(ROWS)]
        for r in range(ROWS):
            total = acc[p, r, h, :]
            for k in range(14):
                if 0 <= r + k - BEFORE < ROWS:
                    total = total + taps[1, k] * v[r + k - BEFORE]
            acc[p, r, h, :] = total
        return carry

    lax.fori_loop(0, PLANES * 2, along_y, 0)

    def along_x(i, carry):
        r, h = i // 2, pl.ds(pl.multiple_of((i % 2) * half, half), half)
        v = [psi[q, r, h, :].astype(F32) for q in range(PLANES)]
        for p in range(PLANES):
            total = acc[p, r, h, :]
            for k in range(14):
                if 0 <= p + k - BEFORE < PLANES:
                    total = total + taps[0, k] * v[p + k - BEFORE]
            acc[p, r, h, :] = total
        return carry

    lax.fori_loop(0, ROWS * 2, along_x, 0)

    def finish(c):
        planes = range(c * NY, (c + 1) * NY)
        lefts = [q for q in range(BEFORE) if any(0 <= q - p < 14 for p in planes)]
        rights = [q for q in range(AFTER) if any(0 <= q + BEFORE + PLANES - p < 14 for p in planes)]

        def body(i, carry):
            r, h = i // 2, pl.ds(pl.multiple_of((i % 2) * half, half), half)
            lv = {q: left[q, r, h, :].astype(F32) for q in lefts}
            rv = {q: right[q, r, h, :].astype(F32) for q in rights}
            for p in planes:
                total = acc[p, r, h, :]
                for q in lefts:
                    k = q - p
                    if 0 <= k < 14:
                        total = total + taps[0, k] * lv[q]
                for q in rights:
                    k = q + BEFORE + PLANES - p
                    if 0 <= k < 14:
                        total = total + taps[0, k] * rv[q]
                img[p, r, h, :] = total.astype(BF16)
            return carry

        lax.fori_loop(0, ROWS * 2, body, 0)

    def slot(b):
        return pl.ds(pl.multiple_of(b * ORB, ORB), ORB)

    def img_copy(k, c):
        to = y_peer(k)
        return remote(
            img.at[c * NY + to], img_all.at[c, :, slot(band), :],
            img_send.at[k, c], img_recv.at[k, c], to * NX + xl, space,
        )

    def fwd_copy(k, c):
        of = lax.rem(y + NY - k, NY) * NX + xl
        src = img.at[c * NY + y] if k == 0 else img_all.at[c, :, slot(of), :]
        return remote(src, img_all.at[c, :, slot(of), :], fwd_send.at[k, c], fwd_recv.at[k, c], partner, space)

    for c in range(CHUNKS):
        if c == 0:

            @pl.when(jnp.logical_not(first))
            def _():
                up.wait_recv()

            @pl.when(jnp.logical_not(last))
            def _():
                down[0].wait_recv()
        else:

            @pl.when(jnp.logical_not(last))
            def _():
                down[1].wait_recv()

        finish(c)
        for k in (2, 1, 3):
            img_copy(k, c).start()
        fwd_copy(0, c).start()
        img_all[c, :, slot(band), :] = img[c * NY + y]

    for k in range(1, NY):
        panel_copy(k).wait_recv()
        for c in range(CHUNKS):
            psi_copy(k, c).wait_recv()

    def rot_copy(k, c):
        to = y_peer(k)
        return remote(
            rot.at[c, :, slot(to), :], out.at[c * NY + y], rot_send.at[k, c], rot_recv.at[k, c], to * NX + xl, space
        )

    kacc[...] = jnp.zeros(kacc.shape, F32)
    for c in range(CHUNKS):
        for k in (1, 3, 2):
            img_copy(k, c).wait_recv()
            fwd_copy(k, c).start()
    for c in range(CHUNKS):
        for k in range(NY):
            fwd_copy(k, c).wait_recv()
        group = 4

        def rotate(i, carry):
            at = i * group
            images = jnp.concatenate([img_all[c, at + j] for j in range(group)], axis=1)
            r = jnp.dot(own_panels[...], images, preferred_element_type=F32).astype(BF16)
            for j in range(group):
                rot[c, at + j] = r[:, j * LANES : (j + 1) * LANES]
            values = jnp.concatenate([psi_all[c, at + j] for j in range(group)], axis=1)
            kacc[...] += lax.dot_general(values, images, (((1,), (1,)), ((), ())), preferred_element_type=F32)
            return carry

        lax.fori_loop(0, ROWS // group, rotate, 0)
        for k in (2, 1, 3):
            rot_copy(k, c).start()
        out[c * NY + y] = rot[c, :, slot(y), :]

    def ky_copy(k):
        to = y_peer(k)
        return remote(kacc.at[slot(to), :], ky.at[k], ky_send.at[k], ky_recv.at[k], to * NX + xl, space)

    for k in range(1, NY):
        ky_copy(k).start()
    for k in range(1, NY):
        ky_copy(k).wait_recv()
    ky[0] = (kacc[slot(y), :] + ky[1]) + (ky[2] + ky[3])
    eight = ORB // NG

    def kg_copy(k):
        to = lax.rem(g + k, NG)
        return remote(
            ky.at[0, pl.ds(pl.multiple_of(to * eight, eight), eight), :], kg.at[k],
            kg_send.at[k], kg_recv.at[k], band, z * NG + to,
        )

    for k in range(1, NG):
        kg_copy(k).start()
    for k in range(1, NG):
        kg_copy(k).wait_recv()
    scale = 1.0 / (slabs * PLANES * ROWS * LANES)
    kzs[...] = ((ky[0, pl.ds(pl.multiple_of(g * eight, eight), eight), :] + kg[1]) + (kg[2] + kg[3])) * scale

    def kz_copy(k):
        return remote(kzs, kz.at[z], kz_send.at[k], kz_recv.at[k], band, lax.rem(z + k, nz) * NG + g)

    def kz_start(k, carry):
        kz_copy(k).start()
        return carry

    def kz_wait(k, carry):
        kz_copy(k).wait_recv()
        return carry

    lax.fori_loop(1, nz, kz_start, 0)
    kz[z] = kzs[...]
    lax.fori_loop(1, nz, kz_wait, 0)
    rows = pl.ds(pl.multiple_of(g * eight, eight), eight)
    total = kz[0]
    for i in range(1, nz):
        total = total + kz[i]
    kin[rows, :] = total

    def ka_copy(k):
        return remote(
            kin.at[rows, :], kin.at[rows, :], ka_send.at[k], ka_recv.at[k], band, z * NG + lax.rem(g + k, NG)
        )

    for k in range(1, NG):
        ka_copy(k).start()
    for k in range(1, NG):
        ka_copy(k).wait_recv()

    for c in range(CHUNKS):
        for k in range(1, NY):
            rot_copy(k, c).wait_recv()

    @pl.when(jnp.logical_not(last))
    def _():
        up.wait_send()

    @pl.when(jnp.logical_not(first))
    def _():
        down[0].wait_send()
        down[1].wait_send()

    for k in range(1, NY):
        panel_copy(k).wait_send()
        ky_copy(k).wait_send()
        for c in range(CHUNKS):
            psi_copy(k, c).wait_send()
            img_copy(k, c).wait_send()
            rot_copy(k, c).wait_send()
    for k in range(NY):
        for c in range(CHUNKS):
            fwd_copy(k, c).wait_send()
    for k in range(1, NG):
        kg_copy(k).wait_send()
        ka_copy(k).wait_send()

    def kz_wait_send(k, carry):
        kz_copy(k).wait_send()
        return carry

    lax.fori_loop(1, nz, kz_wait_send, 0)


def on_device(nz, orbitals, filters, panels):
    psi = jnp.transpose(orbitals, (1, 2, 0, 3))
    vmem = pltpu.VMEM
    dma = pltpu.SemaphoreType.DMA
    eight = ORB // NG
    rotated, kin = pl.pallas_call(
        functools.partial(kernel, nz),
        out_shape=(
            jax.ShapeDtypeStruct((PLANES, ROWS, ORB, LANES), BF16),
            jax.ShapeDtypeStruct((ORB, ALL), F32),
        ),
        in_specs=[
            pl.BlockSpec(memory_space=pltpu.SMEM),
            pl.BlockSpec(memory_space=vmem),
            pl.BlockSpec(memory_space=vmem),
        ],
        out_specs=(pl.BlockSpec(memory_space=vmem), pl.BlockSpec(memory_space=vmem)),
        scratch_shapes=[
            vmem((BEFORE, ROWS, ORB, LANES), BF16),
            vmem((AFTER, ROWS, ORB, LANES), BF16),
            vmem((PLANES, ROWS, ORB, LANES), F32),
            vmem((PLANES, ROWS, ORB, LANES), BF16),
            vmem((CHUNKS, ROWS, ORB * NY, LANES), BF16),
            vmem((CHUNKS, ROWS, ALL, LANES), BF16),
            vmem((CHUNKS, ROWS, ORB * NY, LANES), BF16),
            vmem((ORB * NY, ALL), BF16),
            vmem((ORB * NY, ALL), F32),
            vmem((NY, ORB, ALL), F32),
            vmem((NG, eight, ALL), F32),
            vmem((nz, eight, ALL), F32),
            vmem((eight, ALL), F32),
            vmem((2 * LANES, LANES), BF16),
            dma((3,)), dma((3,)),
            dma((NY, CHUNKS)), dma((NY, CHUNKS)),
            dma((NY,)), dma((NY,)),
            dma((NY, CHUNKS)), dma((NY, CHUNKS)),
            dma((NY, CHUNKS)), dma((NY, CHUNKS)),
            dma((NY, CHUNKS)), dma((NY, CHUNKS)),
            dma((NY,)), dma((NY,)),
            dma((NG,)), dma((NG,)),
            dma((nz,)), dma((nz,)),
            dma((NG,)), dma((NG,)),
        ],
        compiler_params=pltpu.CompilerParams(
            collective_id=0, has_side_effects=True, vmem_limit_bytes=40 * 1024 * 1024
        ),
    )(filters, psi, panels)
    return jnp.transpose(rotated, (2, 0, 1, 3)), kin


def solution(mesh):
    return jax.shard_map(
        functools.partial(on_device, mesh.shape["space"] // NG),
        mesh=mesh,
        in_specs=(P("band", "space", None, None), P(), P("band", None)),
        out_specs=(P("band", "space", None, None), P("band", None)),
        check_vma=False,
    )
```

```python
import functools

import jax
import jax.numpy as jnp
from jax import lax
from jax.experimental import pallas as pl
from jax.experimental.pallas import tpu as pltpu
from jax.sharding import PartitionSpec as P

MESH = pl.DeviceIdType.MESH
F32, BF16 = jnp.float32, jnp.bfloat16
BEFORE, AFTER = 7, 6
NY, NX = 4, 2
BAND = NY * NX
NG = 4
ZQ = 4
ORB, PLANES, ROWS, LANES = 32, 8, 16, 128
ALL = ORB * BAND
PAIR = 2
CHUNKS = PLANES // PAIR
SHARE = ROWS // BAND
FACE = 7
EIGHT = ORB // NG
STEPS = 3
SAME, CROSS = (4, 2, 6), (3, 5, 1, 7)


def band_matrix(taps, row):
    a = lax.broadcasted_iota(jnp.int32, (LANES, LANES), 0)
    b = lax.broadcasted_iota(jnp.int32, (LANES, LANES), 1)
    total = jnp.zeros((LANES, LANES), F32)
    for k in range(14):
        total = jnp.where(a - b == k - BEFORE, taps[row, k], total)
    high = total.astype(BF16)
    low = (total - high.astype(F32)).astype(BF16)
    return jnp.concatenate([high, low], axis=0)


def kernel(
    nz,
    taps, orbitals, panels,
    out, kin,
    psi, psi_p, far, near, acc, img, psi_all, img_all, rot, all_panels, kacc, ktwin, krs, kz1, kz2, kpart, zmat,
    part_send, part_recv, far_send, far_recv, near_send, near_recv, psi_send, psi_recv, pan_send, pan_recv,
    img_send, img_recv, rot_send, rot_recv, ktwin_send, ktwin_recv, krs_send, krs_recv, kz1_send, kz1_recv, kz2_send, kz2_recv, ka_send, ka_recv, known,
):
    band, space = lax.axis_index("band"), lax.axis_index("space")
    y, xl = band // NX, band % NX
    z, g, core = space // NG, space % NG, space % 2
    slabs = nz * NG
    partner = y * NX + (1 - xl)
    twin = space + 1 - 2 * core
    beyond = space - 1 + 2 * core
    inside = jnp.logical_and(beyond >= 0, beyond < slabs)
    layer = BAND * 2
    me = band * 2 + g // 2

    def remote(src, dst, send, recv, b, s):
        return pltpu.make_async_remote_copy(
            src_ref=src, dst_ref=dst, send_sem=send, recv_sem=recv, device_id=(b, s), device_id_type=MESH
        )

    def slot(b):
        return pl.ds(pl.multiple_of(b * ORB, ORB), ORB)

    def share(b):
        return pl.ds((b % NX) * (ROWS // NX) + (b // NX) * SHARE, SHARE)

    def peer(k):
        return lax.rem(band + k, BAND)

    barrier = pltpu.get_barrier_semaphore()

    def greet(b, s):
        pl.semaphore_signal(barrier, inc=1, device_id=(b, s), device_id_type=MESH)

    greet(partner, lax.rem(beyond + slabs, slabs))
    quarter, place = z // ZQ, z % ZQ
    quarters = nz // ZQ

    def z_near(k):
        return (quarter * ZQ + lax.rem(place + k, ZQ)) * NG + g

    def z_far(k):
        return (lax.rem(quarter + k, quarters) * ZQ + place) * NG + g

    def along(k):
        return lax.rem(z + k + nz, nz) * NG + g

    for k in (1, -1):
        greet(band, along(k))

    def in_layer(k):
        to = lax.rem(me + k, layer)
        return to, to // 2, z * NG + (to % 2) * 2 + core

    def greet_layer(k, carry):
        _, b, s = in_layer(k)
        greet(b, s)
        return carry

    lax.fori_loop(1, layer, greet_layer, 0)
    greet(band, twin)
    greet(band, z * NG + lax.rem(g + 2, NG) + 1 - 2 * core)
    size = ROWS * ROWS
    a = lax.broadcasted_iota(jnp.int32, (size, size), 0)
    b = lax.broadcasted_iota(jnp.int32, (size, size), 1)
    swap = jnp.where((a // ROWS == b % ROWS) & (a % ROWS == b // ROWS), 1.0, 0.0).astype(BF16)

    def turn(p, carry):
        for h in range(ORB // ROWS):
            v = orbitals[h * ROWS : (h + 1) * ROWS, p].reshape(size, LANES)
            r = jnp.dot(swap, v, preferred_element_type=F32).astype(BF16)
            psi[p, :, h * ROWS : (h + 1) * ROWS, :] = r.reshape(ROWS, ROWS, LANES)
        return carry

    lax.fori_loop(0, PLANES, turn, 0)
    pl.semaphore_wait(barrier, 1 + 2 + 2 + layer - 1)

    def tell(step):
        for k in (1 << step, -(1 << step)):
            pl.semaphore_signal(known.at[step], inc=1, device_id=(band, along(k)), device_id_type=MESH)

    def hear(step):
        pl.semaphore_wait(known.at[step], 2)

    tell(0)

    def plane(t):
        return t + core * (PLANES - 1 - 2 * t)

    def part_copy(t):
        p = plane(t)
        if t < FACE:
            return remote(psi.at[p], psi_p.at[p], part_send.at[t], part_recv.at[t], partner, space)
        rows = pl.ds((1 - xl) * (ROWS // NX), ROWS // NX)
        return remote(psi.at[p, rows], psi_p.at[p, rows], part_send.at[t], part_recv.at[t], partner, space)

    def far_copy(t):
        return remote(psi_p.at[plane(t)], far.at[t], far_send.at[t], far_recv.at[t], partner, beyond)

    near_copy = remote(psi.at[pl.ds(1 - core, FACE)], near, near_send, near_recv, band, twin)

    for t in range(PLANES):
        part_copy(t).start()
    near_copy.start()

    def psi_copy(k, h):
        to = lax.rem(y + k, NY) * NX + xl
        src, owner = (psi, band) if h == 0 else (psi_p, partner)
        planes = pl.ds(0, PLANES) if h == 0 else pl.ds(PLANES // 2 * (core if h == 1 else 1 - core), PLANES // 2)
        return remote(
            src.at[planes, share(to)], psi_all.at[planes, :, slot(owner), :],
            psi_send.at[k, h], psi_recv.at[k, h], to, space,
        )

    def panel_copy(k):
        return remote(panels, all_panels.at[slot(band), :], pan_send.at[k], pan_recv.at[k], peer(k), space)

    for k in (1, 3, 2):
        psi_copy(k, 0).start()
    all_panels[slot(band), :] = panels[...]
    psi_all[:, :, slot(band), :] = psi[:, share(band)]

    @pl.when(jnp.logical_not(inside))
    def _():
        far[...] = jnp.zeros(far.shape, BF16)

    def relay(t):
        part_copy(t).wait_recv()
        if t < FACE:

            @pl.when(inside)
            def _():
                far_copy(t).start()

    def arrived(t):
        @pl.when(inside)
        def _():
            far_copy(t).wait_recv()

    zmat[...] = band_matrix(taps, 2)

    def along_z(p, carry):
        v = psi[p].reshape(ROWS * ORB, LANES)
        r = jnp.dot(jnp.concatenate([v, v], axis=1), zmat[...], preferred_element_type=F32)
        acc[p] = r.reshape(ROWS, ORB, LANES)
        return carry

    lax.fori_loop(0, PLANES, along_z, 0)
    relay(0)
    half = 16

    def along_y(i, carry):
        p, h = i // 2, pl.ds(pl.multiple_of((i % 2) * half, half), half)
        v = [psi[p, r, h, :].astype(F32) for r in range(ROWS)]
        for r in range(ROWS):
            total = acc[p, r, h, :]
            for k in range(14):
                if 0 <= r + k - BEFORE < ROWS:
                    total = total + taps[1, k] * v[r + k - BEFORE]
            acc[p, r, h, :] = total
        return carry

    lax.fori_loop(0, PLANES * 2, along_y, 0)
    relay(1)

    def along_x(i, carry):
        r, h = i // 2, pl.ds(pl.multiple_of((i % 2) * half, half), half)
        v = [psi[q, r, h, :].astype(F32) for q in range(PLANES)]
        for p in range(PLANES):
            total = acc[p, r, h, :]
            for k in range(14):
                if 0 <= p + k - BEFORE < PLANES:
                    total = total + taps[0, k] * v[p + k - BEFORE]
            acc[p, r, h, :] = total
        return carry

    lax.fori_loop(0, ROWS * 2, along_x, 0)
    relay(2)

    def finish(planes, left, right):
        lefts = [q for q in range(BEFORE) if any(0 <= q - p < 14 for p in planes)]
        rights = [q for q in range(AFTER) if any(0 <= q + BEFORE + PLANES - p < 14 for p in planes)]

        def body(i, carry):
            r, h = i // 2, pl.ds(pl.multiple_of((i % 2) * half, half), half)
            lv = {q: left(q, r, h).astype(F32) for q in lefts}
            rv = {q: right(q, r, h).astype(F32) for q in rights}
            for p in planes:
                total = acc[p, r, h, :]
                for q in lefts:
                    if 0 <= q - p < 14:
                        total = total + taps[0, q - p] * lv[q]
                for q in rights:
                    k = q + BEFORE + PLANES - p
                    if 0 <= k < 14:
                        total = total + taps[0, k] * rv[q]
                img[p, r, h, :] = total.astype(BF16)
            return carry

        lax.fori_loop(0, ROWS * 2, body, 0)

    def pair(j):
        return pl.ds(PLANES - PAIR - PAIR * j + core * (2 * PAIR * j - PLANES + PAIR), PAIR)

    def img_copy(k, j):
        to = peer(k)
        return remote(
            img.at[pair(j), share(to)], img_all.at[pair(j), :, slot(band), :],
            img_send.at[k, j], img_recv.at[k, j], to, space,
        )

    def rot_copy(k, j):
        to = peer(k)
        return remote(
            rot.at[pair(j), :, slot(to), :], out.at[pair(j), share(band)],
            rot_send.at[k, j], rot_recv.at[k, j], to, space,
        )

    def image(j):
        @pl.when(core == 0)
        def _():
            finish(
                (PLANES - PAIR * (j + 1), PLANES - PAIR * j - 1),
                lambda q, r, h: far[BEFORE - 1 - q, r, h, :],
                lambda q, r, h: near[q, r, h, :],
            )

        @pl.when(core == 1)
        def _():
            finish(
                (PAIR * j, PAIR * j + 1),
                lambda q, r, h: near[q, r, h, :],
                lambda q, r, h: far[q, r, h, :],
            )

        for k in SAME:
            img_copy(k, j).start()
        img_all[pair(j), :, slot(band), :] = img[pair(j), share(band)]

    def spread(ref, j):
        v = ref[pair(j)]
        return jnp.concatenate([v[a, b] for a in range(PAIR) for b in range(SHARE)], axis=1)

    def rotate(j):
        r = jnp.dot(all_panels[...], spread(img_all, j), preferred_element_type=F32).astype(BF16)
        parts = [r[:, i * LANES : (i + 1) * LANES] for i in range(PAIR * SHARE)]
        rot[pair(j)] = jnp.stack(parts).reshape(PAIR, SHARE, ALL, LANES)

    def kinetic(j):
        r = lax.dot_general(
            spread(psi_all, j), spread(img_all, j), (((1,), (1,)), ((), ())), preferred_element_type=F32
        ).reshape(kacc.shape)
        kacc[...] = r if j == 0 else kacc[...] + r

    near_copy.wait_recv()
    hear(0)
    tell(1)
    arrived(0)
    image(0)
    relay(3)
    for k in (1, 3, 2):
        psi_copy(k, 1).start()
    relay(4)
    hear(1)
    tell(2)
    arrived(1)
    arrived(2)
    image(1)
    relay(5)
    relay(6)
    arrived(3)
    arrived(4)
    image(2)
    relay(7)
    for k in (1, 3, 2):
        psi_copy(k, 2).start()
    for t in range(PLANES):
        part_copy(t).wait_send()
    for j in range(CHUNKS - 1):
        for k in CROSS:
            img_copy(k, j).start()
    psi_all[:, :, slot(partner), :] = psi_p[:, share(band)]
    arrived(5)
    arrived(6)
    image(3)
    for k in CROSS:
        img_copy(k, CHUNKS - 1).start()
    for k in SAME + CROSS:
        panel_copy(k).start()

    for k in range(1, NY):
        for h in range(3):
            psi_copy(k, h).wait_recv()
    for j in range(CHUNKS):
        for k in range(1, BAND):
            img_copy(k, j).wait_recv()
        kinetic(j)

    def krs_copy(k):
        to, b, s = in_layer(k)
        return remote(ktwin.at[to], krs.at[k], krs_send.at[k], krs_recv.at[k], b, s)

    twin_copy = remote(kacc.at[:, 1 - core], ktwin, ktwin_send, ktwin_recv, band, twin)
    twin_copy.start()
    twin_copy.wait_recv()
    ktwin[...] += kacc[:, core]

    def krs_start(k, carry):
        krs_copy(k).start()
        return carry

    def krs_wait(k, carry):
        krs_copy(k).wait_recv()
        return carry

    lax.fori_loop(1, layer, krs_start, 0)


    def cross(j):
        for k in CROSS:
            rot_copy(k, j).start()

    for k in range(1, BAND):
        panel_copy(k).wait_recv()
    for j in range(CHUNKS):
        rotate(j)
        for k in SAME:
            rot_copy(k, j).start()
        if j < 2:
            cross(j)
    for j in range(CHUNKS):
        out[pair(j), share(band)] = rot[pair(j), :, slot(band), :]
    krs[0] = ktwin[me]
    lax.fori_loop(1, layer, krs_wait, 0)
    scale = 1.0 / (slabs * PLANES * ROWS * LANES)
    kpart[0] = jnp.sum(krs[...], axis=0) * scale

    def kz1_copy(k):
        return remote(kpart.at[0], kz1.at[place], kz1_send.at[k], kz1_recv.at[k], band, z_near(k))

    def kz2_copy(k):
        return remote(kpart.at[1], kz2.at[quarter], kz2_send.at[k], kz2_recv.at[k], band, z_far(k))

    hear(2)
    for k in range(1, ZQ):
        kz1_copy(k).start()
    cross(2)
    kz1[place] = kpart[0]
    for k in range(1, ZQ):
        kz1_copy(k).wait_recv()
    kpart[1] = jnp.sum(kz1[...], axis=0)
    for k in range(1, quarters):
        kz2_copy(k).start()
    cross(3)
    kz2[quarter] = kpart[1]
    for k in range(1, quarters):
        kz2_copy(k).wait_recv()
    rows = pl.ds(pl.multiple_of(g * EIGHT, EIGHT), EIGHT)
    kin[rows, :] = jnp.sum(kz2[...], axis=0)

    def ka_copy(k):
        return remote(
            kin.at[rows, :], kin.at[rows, :], ka_send.at[k], ka_recv.at[k], band, z * NG + lax.rem(g + k, NG)
        )

    for k in range(1, NG):
        ka_copy(k).start()
    for k in range(1, NG):
        ka_copy(k).wait_recv()
    for j in range(CHUNKS):
        for k in range(1, BAND):
            rot_copy(k, j).wait_recv()

    @pl.when(inside)
    def _():
        for t in range(FACE):
            far_copy(t).wait_send()

    near_copy.wait_send()
    for k in range(1, NY):
        for h in range(3):
            psi_copy(k, h).wait_send()
    for k in range(1, BAND):
        panel_copy(k).wait_send()
        for j in range(CHUNKS):
            img_copy(k, j).wait_send()
            rot_copy(k, j).wait_send()

    def krs_sent(k, carry):
        krs_copy(k).wait_send()
        return carry

    twin_copy.wait_send()
    lax.fori_loop(1, layer, krs_sent, 0)
    for k in range(1, ZQ):
        kz1_copy(k).wait_send()
    for k in range(1, quarters):
        kz2_copy(k).wait_send()
    for k in range(1, NG):
        ka_copy(k).wait_send()


def on_device(nz, orbitals, filters, panels):
    vmem = pltpu.VMEM
    dma = pltpu.SemaphoreType.DMA
    slab = (PLANES, ROWS, ORB, LANES)
    mixed = (PLANES, SHARE, ALL, LANES)
    layer = BAND * 2
    rotated, kin = pl.pallas_call(
        functools.partial(kernel, nz),
        out_shape=(jax.ShapeDtypeStruct(slab, BF16), jax.ShapeDtypeStruct((ORB, ALL), F32)),
        in_specs=[
            pl.BlockSpec(memory_space=pltpu.SMEM),
            pl.BlockSpec(memory_space=vmem),
            pl.BlockSpec(memory_space=vmem),
        ],
        out_specs=(pl.BlockSpec(memory_space=vmem), pl.BlockSpec(memory_space=vmem)),
        scratch_shapes=[
            vmem(slab, BF16),
            vmem(slab, BF16),
            vmem((FACE, ROWS, ORB, LANES), BF16),
            vmem((FACE, ROWS, ORB, LANES), BF16),
            vmem(slab, F32),
            vmem(slab, BF16),
            vmem(mixed, BF16),
            vmem(mixed, BF16),
            vmem(mixed, BF16),
            vmem((ALL, ALL), BF16),
            vmem((BAND * 2, 2, EIGHT, ALL), F32),
            vmem((BAND * 2, EIGHT, ALL), F32),
            vmem((layer, EIGHT, ALL), F32),
            vmem((ZQ, EIGHT, ALL), F32),
            vmem((nz // ZQ, EIGHT, ALL), F32),
            vmem((2, EIGHT, ALL), F32),
            vmem((2 * LANES, LANES), BF16),
            dma((PLANES,)), dma((PLANES,)),
            dma((FACE,)), dma((FACE,)),
            dma, dma,
            dma((NY, 3)), dma((NY, 3)),
            dma((BAND,)), dma((BAND,)),
            dma((BAND, CHUNKS)), dma((BAND, CHUNKS)),
            dma((BAND, CHUNKS)), dma((BAND, CHUNKS)),
            dma, dma,
            dma((layer,)), dma((layer,)),
            dma((ZQ,)), dma((ZQ,)),
            dma((nz // ZQ,)), dma((nz // ZQ,)),
            dma((NG,)), dma((NG,)),
            pltpu.SemaphoreType.REGULAR((STEPS,)),
        ],
        compiler_params=pltpu.CompilerParams(
            collective_id=0, has_side_effects=True, vmem_limit_bytes=40 * 1024 * 1024
        ),
    )(filters, orbitals, panels)
    return jnp.transpose(rotated, (2, 0, 1, 3)), kin


def solution(mesh):
    return jax.shard_map(
        functools.partial(on_device, mesh.shape["space"] // NG),
        mesh=mesh,
        in_specs=(P("band", "space", None, None), P(), P("band", None)),
        out_specs=(P("band", "space", None, None), P("band", None)),
        check_vma=False,
    )
```

```python
import functools

import jax
import jax.numpy as jnp
from jax import lax
from jax.experimental import pallas as pl
from jax.experimental.pallas import tpu as pltpu
from jax.sharding import PartitionSpec as P

MESH = pl.DeviceIdType.MESH
F32, BF16 = jnp.float32, jnp.bfloat16
BEFORE, AFTER = 7, 6
NY, NX = 4, 2
BAND = NY * NX
NG = 4
ZQ = 4
ORB, PLANES, ROWS, LANES = 32, 8, 16, 128
ALL = ORB * BAND
SIZES = (2, 2, 2, 1, 1)
CHUNKS = len(SIZES)
SHARE = ROWS // BAND
FACE = 7
EIGHT = ORB // NG
STEPS = 3
SAME, CROSS = (4, 2, 6), (3, 5, 1, 7)


def band_matrix(taps, row):
    a = lax.broadcasted_iota(jnp.int32, (LANES, LANES), 0)
    b = lax.broadcasted_iota(jnp.int32, (LANES, LANES), 1)
    total = jnp.zeros((LANES, LANES), F32)
    for k in range(14):
        total = jnp.where(a - b == k - BEFORE, taps[row, k], total)
    high = total.astype(BF16)
    low = (total - high.astype(F32)).astype(BF16)
    return jnp.concatenate([high, low], axis=0)


def kernel(
    nz,
    taps, orbitals, panels,
    out, kin,
    psi, psi_p, far, near, acc, img, psi_all, img_all, rot, all_panels, kacc, ktwin, krs, kz1, kz2, kpart, zmat,
    part_send, part_recv, far_send, far_recv, near_send, near_recv, psi_send, psi_recv, pan_send, pan_recv,
    img_send, img_recv, rot_send, rot_recv, ktwin_send, ktwin_recv, krs_send, krs_recv, kz1_send, kz1_recv, kz2_send, kz2_recv, ka_send, ka_recv, known,
):
    band, space = lax.axis_index("band"), lax.axis_index("space")
    y, xl = band // NX, band % NX
    z, g, core = space // NG, space % NG, space % 2
    slabs = nz * NG
    partner = y * NX + (1 - xl)
    twin = space + 1 - 2 * core
    beyond = space - 1 + 2 * core
    inside = jnp.logical_and(beyond >= 0, beyond < slabs)
    layer = BAND * 2
    me = band * 2 + g // 2

    def remote(src, dst, send, recv, b, s):
        return pltpu.make_async_remote_copy(
            src_ref=src, dst_ref=dst, send_sem=send, recv_sem=recv, device_id=(b, s), device_id_type=MESH
        )

    def slot(b):
        return pl.ds(pl.multiple_of(b * ORB, ORB), ORB)

    def share(b):
        return pl.ds((b % NX) * (ROWS // NX) + (b // NX) * SHARE, SHARE)

    def peer(k):
        return lax.rem(band + k, BAND)

    barrier = pltpu.get_barrier_semaphore()

    def greet(b, s):
        pl.semaphore_signal(barrier, inc=1, device_id=(b, s), device_id_type=MESH)

    greet(partner, lax.rem(beyond + slabs, slabs))
    quarter, place = z // ZQ, z % ZQ
    quarters = nz // ZQ

    def z_near(k):
        return (quarter * ZQ + lax.rem(place + k, ZQ)) * NG + g

    def z_far(k):
        return (lax.rem(quarter + k, quarters) * ZQ + place) * NG + g

    def along(k):
        return lax.rem(z + k + nz, nz) * NG + g

    for k in (1, -1):
        greet(band, along(k))

    def in_layer(k):
        to = lax.rem(me + k, layer)
        return to, to // 2, z * NG + (to % 2) * 2 + core

    def greet_layer(k, carry):
        _, b, s = in_layer(k)
        greet(b, s)
        return carry

    lax.fori_loop(1, layer, greet_layer, 0)
    greet(band, twin)
    greet(band, z * NG + lax.rem(g + 2, NG) + 1 - 2 * core)
    size = ROWS * ROWS
    a = lax.broadcasted_iota(jnp.int32, (size, size), 0)
    b = lax.broadcasted_iota(jnp.int32, (size, size), 1)
    swap = jnp.where((a // ROWS == b % ROWS) & (a % ROWS == b // ROWS), 1.0, 0.0).astype(BF16)

    def turn(p, carry):
        for h in range(ORB // ROWS):
            v = orbitals[h * ROWS : (h + 1) * ROWS, p].reshape(size, LANES)
            r = jnp.dot(swap, v, preferred_element_type=F32).astype(BF16)
            psi[p, :, h * ROWS : (h + 1) * ROWS, :] = r.reshape(ROWS, ROWS, LANES)
        return carry

    lax.fori_loop(0, PLANES, turn, 0)
    pl.semaphore_wait(barrier, 1 + 2 + 2 + layer - 1)

    def tell(step):
        for k in (1 << step, -(1 << step)):
            pl.semaphore_signal(known.at[step], inc=1, device_id=(band, along(k)), device_id_type=MESH)

    def hear(step):
        pl.semaphore_wait(known.at[step], 2)

    tell(0)

    def plane(t):
        return t + core * (PLANES - 1 - 2 * t)

    def part_copy(t):
        p = plane(t)
        if t < FACE:
            return remote(psi.at[p], psi_p.at[p], part_send.at[t], part_recv.at[t], partner, space)
        rows = pl.ds((1 - xl) * (ROWS // NX), ROWS // NX)
        return remote(psi.at[p, rows], psi_p.at[p, rows], part_send.at[t], part_recv.at[t], partner, space)

    def far_copy(t):
        return remote(psi_p.at[plane(t)], far.at[t], far_send.at[t], far_recv.at[t], partner, beyond)

    near_copy = remote(psi.at[pl.ds(1 - core, FACE)], near, near_send, near_recv, band, twin)

    for t in range(PLANES):
        part_copy(t).start()
    near_copy.start()

    def psi_copy(k, h):
        to = lax.rem(y + k, NY) * NX + xl
        src, owner = (psi, band) if h == 0 else (psi_p, partner)
        first, count = ((0, PLANES), (0, 4), (4, 2), (6, 2))[h]
        planes = pl.ds(first + core * (PLANES - count - 2 * first), count) if h else pl.ds(0, PLANES)
        return remote(
            src.at[planes, share(to)], psi_all.at[planes, :, slot(owner), :],
            psi_send.at[k, h], psi_recv.at[k, h], to, space,
        )

    def panel_copy(k):
        return remote(panels, all_panels.at[slot(band), :], pan_send.at[k], pan_recv.at[k], peer(k), space)

    for k in (1, 3, 2):
        psi_copy(k, 0).start()
    all_panels[slot(band), :] = panels[...]
    psi_all[:, :, slot(band), :] = psi[:, share(band)]

    @pl.when(jnp.logical_not(inside))
    def _():
        far[...] = jnp.zeros(far.shape, BF16)

    def relay(t):
        part_copy(t).wait_recv()
        if t < FACE:

            @pl.when(inside)
            def _():
                far_copy(t).start()

    def arrived(t):
        @pl.when(inside)
        def _():
            far_copy(t).wait_recv()

    zmat[...] = band_matrix(taps, 2)

    def along_z(p, carry):
        v = psi[p].reshape(ROWS * ORB, LANES)
        r = jnp.dot(jnp.concatenate([v, v], axis=1), zmat[...], preferred_element_type=F32)
        acc[p] = r.reshape(ROWS, ORB, LANES)
        return carry

    lax.fori_loop(0, PLANES, along_z, 0)
    relay(0)
    half = 16

    def along_y(i, carry):
        p, h = i // 2, pl.ds(pl.multiple_of((i % 2) * half, half), half)
        v = [psi[p, r, h, :].astype(F32) for r in range(ROWS)]
        for r in range(ROWS):
            total = acc[p, r, h, :]
            for k in range(14):
                if 0 <= r + k - BEFORE < ROWS:
                    total = total + taps[1, k] * v[r + k - BEFORE]
            acc[p, r, h, :] = total
        return carry

    lax.fori_loop(0, PLANES * 2, along_y, 0)
    relay(1)

    def along_x(i, carry):
        r, h = i // 2, pl.ds(pl.multiple_of((i % 2) * half, half), half)
        v = [psi[q, r, h, :].astype(F32) for q in range(PLANES)]
        for p in range(PLANES):
            total = acc[p, r, h, :]
            for k in range(14):
                if 0 <= p + k - BEFORE < PLANES:
                    total = total + taps[0, k] * v[p + k - BEFORE]
            acc[p, r, h, :] = total
        return carry

    lax.fori_loop(0, ROWS * 2, along_x, 0)
    relay(2)

    def finish(planes, left, right):
        lefts = [q for q in range(BEFORE) if any(0 <= q - p < 14 for p in planes)]
        rights = [q for q in range(AFTER) if any(0 <= q + BEFORE + PLANES - p < 14 for p in planes)]

        def body(i, carry):
            r, h = i // 2, pl.ds(pl.multiple_of((i % 2) * half, half), half)
            lv = {q: left(q, r, h).astype(F32) for q in lefts}
            rv = {q: right(q, r, h).astype(F32) for q in rights}
            for p in planes:
                total = acc[p, r, h, :]
                for q in lefts:
                    if 0 <= q - p < 14:
                        total = total + taps[0, q - p] * lv[q]
                for q in rights:
                    k = q + BEFORE + PLANES - p
                    if 0 <= k < 14:
                        total = total + taps[0, k] * rv[q]
                img[p, r, h, :] = total.astype(BF16)
            return carry

        lax.fori_loop(0, ROWS * 2, body, 0)

    def pair(j):
        done, count = sum(SIZES[:j]), SIZES[j]
        return pl.ds(PLANES - done - count + core * (2 * done + count - PLANES), count)

    def img_copy(k, j):
        to = peer(k)
        return remote(
            img.at[pair(j), share(to)], img_all.at[pair(j), :, slot(band), :],
            img_send.at[k, j], img_recv.at[k, j], to, space,
        )

    def rot_copy(k, j):
        to = peer(k)
        return remote(
            rot.at[pair(j), :, slot(to), :], out.at[pair(j), share(band)],
            rot_send.at[k, j], rot_recv.at[k, j], to, space,
        )

    def image(j):
        @pl.when(core == 0)
        def _():
            finish(
                range(PLANES - sum(SIZES[: j + 1]), PLANES - sum(SIZES[:j])),
                lambda q, r, h: far[BEFORE - 1 - q, r, h, :],
                lambda q, r, h: near[q, r, h, :],
            )

        @pl.when(core == 1)
        def _():
            finish(
                range(sum(SIZES[:j]), sum(SIZES[: j + 1])),
                lambda q, r, h: near[q, r, h, :],
                lambda q, r, h: far[q, r, h, :],
            )

        for k in SAME + CROSS:
            img_copy(k, j).start()
        img_all[pair(j), :, slot(band), :] = img[pair(j), share(band)]

    def spread(ref, j):
        v = ref[pair(j)]
        return jnp.concatenate([v[a, b] for a in range(SIZES[j]) for b in range(SHARE)], axis=1)

    def rotate(j):
        r = jnp.dot(all_panels[...], spread(img_all, j), preferred_element_type=F32).astype(BF16)
        parts = [r[:, i * LANES : (i + 1) * LANES] for i in range(SIZES[j] * SHARE)]
        rot[pair(j)] = jnp.stack(parts).reshape(SIZES[j], SHARE, ALL, LANES)

    def kinetic(j):
        r = lax.dot_general(
            spread(psi_all, j), spread(img_all, j), (((1,), (1,)), ((), ())), preferred_element_type=F32
        ).reshape(kacc.shape)
        kacc[...] = r if j == 0 else kacc[...] + r

    near_copy.wait_recv()
    arrived(0)
    image(0)
    relay(3)
    for k in (1, 3, 2):
        psi_copy(k, 1).start()
    relay(4)
    arrived(1)
    arrived(2)
    image(1)
    hear(0)
    tell(1)
    relay(5)
    relay(6)
    for k in (1, 3, 2):
        psi_copy(k, 2).start()
    arrived(3)
    arrived(4)
    image(2)
    relay(7)
    for k in (1, 3, 2):
        psi_copy(k, 3).start()
    psi_all[:, :, slot(partner), :] = psi_p[:, share(band)]
    arrived(5)
    image(3)
    arrived(6)
    image(4)
    hear(1)
    tell(2)
    for k in SAME + CROSS:
        panel_copy(k).start()

    for k in range(1, NY):
        for h in range(4):
            psi_copy(k, h).wait_recv()
    for j in range(CHUNKS):
        for k in range(1, BAND):
            img_copy(k, j).wait_recv()
        kinetic(j)

    def krs_copy(k):
        to, b, s = in_layer(k)
        return remote(ktwin.at[to], krs.at[k], krs_send.at[k], krs_recv.at[k], b, s)

    twin_copy = remote(kacc.at[:, 1 - core], ktwin, ktwin_send, ktwin_recv, band, twin)
    twin_copy.start()
    twin_copy.wait_recv()
    ktwin[...] += kacc[:, core]

    def krs_start(k, carry):
        krs_copy(k).start()
        return carry

    def krs_wait(k, carry):
        krs_copy(k).wait_recv()
        return carry

    lax.fori_loop(1, layer, krs_start, 0)


    for k in range(1, BAND):
        panel_copy(k).wait_recv()

    def turn_out(j):
        rotate(j)
        for k in SAME + CROSS:
            rot_copy(k, j).start()
        out[pair(j), share(band)] = rot[pair(j), :, slot(band), :]

    turn_out(0)
    turn_out(1)
    krs[0] = ktwin[me]
    lax.fori_loop(1, layer, krs_wait, 0)
    scale = 1.0 / (slabs * PLANES * ROWS * LANES)
    kpart[0] = jnp.sum(krs[...], axis=0) * scale

    def kz1_copy(k):
        return remote(kpart.at[0], kz1.at[place], kz1_send.at[k], kz1_recv.at[k], band, z_near(k))

    def kz2_copy(k):
        return remote(kpart.at[1], kz2.at[quarter], kz2_send.at[k], kz2_recv.at[k], band, z_far(k))

    hear(2)
    for k in range(1, ZQ):
        kz1_copy(k).start()
    turn_out(2)
    kz1[place] = kpart[0]
    for k in range(1, ZQ):
        kz1_copy(k).wait_recv()
    kpart[1] = jnp.sum(kz1[...], axis=0)
    for k in range(1, quarters):
        kz2_copy(k).start()
    turn_out(3)
    turn_out(4)
    kz2[quarter] = kpart[1]
    for k in range(1, quarters):
        kz2_copy(k).wait_recv()
    rows = pl.ds(pl.multiple_of(g * EIGHT, EIGHT), EIGHT)
    kin[rows, :] = jnp.sum(kz2[...], axis=0)

    def ka_copy(k):
        return remote(
            kin.at[rows, :], kin.at[rows, :], ka_send.at[k], ka_recv.at[k], band, z * NG + lax.rem(g + k, NG)
        )

    for k in range(1, NG):
        ka_copy(k).start()
    for k in range(1, NG):
        ka_copy(k).wait_recv()
    for j in range(CHUNKS):
        for k in range(1, BAND):
            rot_copy(k, j).wait_recv()

    for t in range(PLANES):
        part_copy(t).wait_send()
    @pl.when(inside)
    def _():
        for t in range(FACE):
            far_copy(t).wait_send()

    near_copy.wait_send()
    for k in range(1, NY):
        for h in range(4):
            psi_copy(k, h).wait_send()
    for k in range(1, BAND):
        panel_copy(k).wait_send()
        for j in range(CHUNKS):
            img_copy(k, j).wait_send()
            rot_copy(k, j).wait_send()

    def krs_sent(k, carry):
        krs_copy(k).wait_send()
        return carry

    twin_copy.wait_send()
    lax.fori_loop(1, layer, krs_sent, 0)
    for k in range(1, ZQ):
        kz1_copy(k).wait_send()
    for k in range(1, quarters):
        kz2_copy(k).wait_send()
    for k in range(1, NG):
        ka_copy(k).wait_send()


def on_device(nz, orbitals, filters, panels):
    vmem = pltpu.VMEM
    dma = pltpu.SemaphoreType.DMA
    slab = (PLANES, ROWS, ORB, LANES)
    mixed = (PLANES, SHARE, ALL, LANES)
    layer = BAND * 2
    rotated, kin = pl.pallas_call(
        functools.partial(kernel, nz),
        out_shape=(jax.ShapeDtypeStruct(slab, BF16), jax.ShapeDtypeStruct((ORB, ALL), F32)),
        in_specs=[
            pl.BlockSpec(memory_space=pltpu.SMEM),
            pl.BlockSpec(memory_space=vmem),
            pl.BlockSpec(memory_space=vmem),
        ],
        out_specs=(pl.BlockSpec(memory_space=vmem), pl.BlockSpec(memory_space=vmem)),
        scratch_shapes=[
            vmem(slab, BF16),
            vmem(slab, BF16),
            vmem((FACE, ROWS, ORB, LANES), BF16),
            vmem((FACE, ROWS, ORB, LANES), BF16),
            vmem(slab, F32),
            vmem(slab, BF16),
            vmem(mixed, BF16),
            vmem(mixed, BF16),
            vmem(mixed, BF16),
            vmem((ALL, ALL), BF16),
            vmem((BAND * 2, 2, EIGHT, ALL), F32),
            vmem((BAND * 2, EIGHT, ALL), F32),
            vmem((layer, EIGHT, ALL), F32),
            vmem((ZQ, EIGHT, ALL), F32),
            vmem((nz // ZQ, EIGHT, ALL), F32),
            vmem((2, EIGHT, ALL), F32),
            vmem((2 * LANES, LANES), BF16),
            dma((PLANES,)), dma((PLANES,)),
            dma((FACE,)), dma((FACE,)),
            dma, dma,
            dma((NY, 4)), dma((NY, 4)),
            dma((BAND,)), dma((BAND,)),
            dma((BAND, CHUNKS)), dma((BAND, CHUNKS)),
            dma((BAND, CHUNKS)), dma((BAND, CHUNKS)),
            dma, dma,
            dma((layer,)), dma((layer,)),
            dma((ZQ,)), dma((ZQ,)),
            dma((nz // ZQ,)), dma((nz // ZQ,)),
            dma((NG,)), dma((NG,)),
            pltpu.SemaphoreType.REGULAR((STEPS,)),
        ],
        compiler_params=pltpu.CompilerParams(
            collective_id=0, has_side_effects=True, vmem_limit_bytes=40 * 1024 * 1024
        ),
    )(filters, orbitals, panels)
    return jnp.transpose(rotated, (2, 0, 1, 3)), kin


def solution(mesh):
    return jax.shard_map(
        functools.partial(on_device, mesh.shape["space"] // NG),
        mesh=mesh,
        in_specs=(P("band", "space", None, None), P(), P("band", None)),
        out_specs=(P("band", "space", None, None), P("band", None)),
        check_vma=False,
    )
```

```python
import functools

import jax
import jax.numpy as jnp
from jax import lax
from jax.experimental import pallas as pl
from jax.experimental.pallas import tpu as pltpu
from jax.sharding import PartitionSpec as P

MESH = pl.DeviceIdType.MESH
F32, BF16 = jnp.float32, jnp.bfloat16
BEFORE, AFTER = 7, 6
NY, NX = 4, 2
BAND = NY * NX
NG = 4
ORB, PLANES, ROWS, LANES = 32, 8, 16, 128
ALL = ORB * BAND
SIZES = (2, 2, 2, 1, 1)
CHUNKS = len(SIZES)
SHARE = ROWS // BAND
FACE = 7
EIGHT = ORB // NG
STEPS = 3
SAME, CROSS = (4, 2, 6), (3, 5, 1, 7)


def band_matrix(taps, row):
    a = lax.broadcasted_iota(jnp.int32, (LANES, LANES), 0)
    b = lax.broadcasted_iota(jnp.int32, (LANES, LANES), 1)
    total = jnp.zeros((LANES, LANES), F32)
    for k in range(14):
        total = jnp.where(a - b == k - BEFORE, taps[row, k], total)
    high = total.astype(BF16)
    low = (total - high.astype(F32)).astype(BF16)
    return jnp.concatenate([high, low], axis=0)


def kernel(
    nz,
    taps, orbitals_in, panels_in,
    out, kin,
    orbitals, panels, psi, psi_p, far, near, acc, img, psi_all, img_all, rot, all_panels, kacc, ktwin, krs, kz, kpart, zmat,
    part_send, part_recv, far_send, far_recv, near_send, near_recv, psi_send, psi_recv, pan_send, pan_recv,
    img_send, img_recv, rot_send, rot_recv, ktwin_send, ktwin_recv, krs_send, krs_recv, kz_send, kz_recv, ka_send, ka_recv, known, load, keep,
):
    band, space = lax.axis_index("band"), lax.axis_index("space")
    y, xl = band // NX, band % NX
    z, g, core = space // NG, space % NG, space % 2
    slabs = nz * NG
    partner = y * NX + (1 - xl)
    twin = space + 1 - 2 * core
    beyond = space - 1 + 2 * core
    inside = jnp.logical_and(beyond >= 0, beyond < slabs)
    layer = BAND * 2
    me = band * 2 + g // 2

    def remote(src, dst, send, recv, b, s):
        return pltpu.make_async_remote_copy(
            src_ref=src, dst_ref=dst, send_sem=send, recv_sem=recv, device_id=(b, s), device_id_type=MESH
        )

    def slot(b):
        return pl.ds(pl.multiple_of(b * ORB, ORB), ORB)

    def share(b):
        return pl.ds((b % NX) * (ROWS // NX) + (b // NX) * SHARE, SHARE)

    def peer(k):
        return lax.rem(band + k, BAND)

    loads = [
        pltpu.make_async_copy(orbitals_in, orbitals, load.at[0]),
        pltpu.make_async_copy(panels_in, panels, load.at[1]),
    ]
    for copy in loads:
        copy.start()

    barrier = pltpu.get_barrier_semaphore()

    def greet(b, s):
        pl.semaphore_signal(barrier, inc=1, device_id=(b, s), device_id_type=MESH)

    greet(partner, lax.rem(beyond + slabs, slabs))
    def along(k):
        return lax.rem(z + k + nz, nz) * NG + g

    for k in (1, -1):
        greet(band, along(k))

    def in_layer(k):
        to = lax.rem(me + k, layer)
        return to, to // 2, z * NG + (to % 2) * 2 + core

    def greet_layer(k, carry):
        _, b, s = in_layer(k)
        greet(b, s)
        return carry

    lax.fori_loop(1, layer, greet_layer, 0)
    greet(band, twin)
    greet(band, z * NG + lax.rem(g + 2, NG) + 1 - 2 * core)
    size = ROWS * ROWS
    a = lax.broadcasted_iota(jnp.int32, (size, size), 0)
    b = lax.broadcasted_iota(jnp.int32, (size, size), 1)
    swap = jnp.where((a // ROWS == b % ROWS) & (a % ROWS == b // ROWS), 1.0, 0.0).astype(BF16)

    def turn(p, carry):
        for h in range(ORB // ROWS):
            v = orbitals[h * ROWS : (h + 1) * ROWS, p].reshape(size, LANES)
            r = jnp.dot(swap, v, preferred_element_type=F32).astype(BF16)
            psi[p, :, h * ROWS : (h + 1) * ROWS, :] = r.reshape(ROWS, ROWS, LANES)
        return carry

    loads[0].wait()
    lax.fori_loop(0, PLANES, turn, 0)
    loads[1].wait()
    pl.semaphore_wait(barrier, 1 + 2 + 2 + layer - 1)

    def tell(step):
        for k in (1 << step, -(1 << step)):
            pl.semaphore_signal(known.at[step], inc=1, device_id=(band, along(k)), device_id_type=MESH)

    def hear(step):
        pl.semaphore_wait(known.at[step], 2)

    tell(0)

    def plane(t):
        return t + core * (PLANES - 1 - 2 * t)

    def part_copy(t):
        p = plane(t)
        if t < FACE:
            return remote(psi.at[p], psi_p.at[p], part_send.at[t], part_recv.at[t], partner, space)
        rows = pl.ds((1 - xl) * (ROWS // NX), ROWS // NX)
        return remote(psi.at[p, rows], psi_p.at[p, rows], part_send.at[t], part_recv.at[t], partner, space)

    def far_copy(t):
        return remote(psi_p.at[plane(t)], far.at[t], far_send.at[t], far_recv.at[t], partner, beyond)

    near_copy = remote(psi.at[pl.ds(1 - core, FACE)], near, near_send, near_recv, band, twin)

    for t in range(PLANES):
        part_copy(t).start()
    near_copy.start()

    def psi_copy(k, h):
        to = lax.rem(y + k, NY) * NX + xl
        src, owner = (psi, band) if h == 0 else (psi_p, partner)
        first, count = ((0, PLANES), (0, 4), (4, 2), (6, 2))[h]
        planes = pl.ds(first + core * (PLANES - count - 2 * first), count) if h else pl.ds(0, PLANES)
        return remote(
            src.at[planes, share(to)], psi_all.at[planes, :, slot(owner), :],
            psi_send.at[k, h], psi_recv.at[k, h], to, space,
        )

    def panel_copy(k):
        return remote(panels, all_panels.at[slot(band), :], pan_send.at[k], pan_recv.at[k], peer(k), space)

    for k in (1, 3, 2):
        psi_copy(k, 0).start()
    all_panels[slot(band), :] = panels[...]
    psi_all[:, :, slot(band), :] = psi[:, share(band)]

    @pl.when(jnp.logical_not(inside))
    def _():
        far[...] = jnp.zeros(far.shape, BF16)

    def relay(t):
        part_copy(t).wait_recv()
        if t < FACE:

            @pl.when(inside)
            def _():
                far_copy(t).start()

    def arrived(t):
        @pl.when(inside)
        def _():
            far_copy(t).wait_recv()

    zmat[...] = band_matrix(taps, 2)

    def along_z(p, carry):
        v = psi[p].reshape(ROWS * ORB, LANES)
        r = jnp.dot(jnp.concatenate([v, v], axis=1), zmat[...], preferred_element_type=F32)
        acc[p] = r.reshape(ROWS, ORB, LANES)
        return carry

    lax.fori_loop(0, PLANES, along_z, 0)
    relay(0)
    half = 16

    def along_y(i, carry):
        p, h = i // 2, pl.ds(pl.multiple_of((i % 2) * half, half), half)
        v = [psi[p, r, h, :].astype(F32) for r in range(ROWS)]
        for r in range(ROWS):
            total = acc[p, r, h, :]
            for k in range(14):
                if 0 <= r + k - BEFORE < ROWS:
                    total = total + taps[1, k] * v[r + k - BEFORE]
            acc[p, r, h, :] = total
        return carry

    lax.fori_loop(0, PLANES * 2, along_y, 0)
    relay(1)

    def along_x(i, carry):
        r, h = i // 2, pl.ds(pl.multiple_of((i % 2) * half, half), half)
        v = [psi[q, r, h, :].astype(F32) for q in range(PLANES)]
        for p in range(PLANES):
            total = acc[p, r, h, :]
            for k in range(14):
                if 0 <= p + k - BEFORE < PLANES:
                    total = total + taps[0, k] * v[p + k - BEFORE]
            acc[p, r, h, :] = total
        return carry

    lax.fori_loop(0, ROWS * 2, along_x, 0)
    relay(2)

    def finish(planes, left, right):
        lefts = [q for q in range(BEFORE) if any(0 <= q - p < 14 for p in planes)]
        rights = [q for q in range(AFTER) if any(0 <= q + BEFORE + PLANES - p < 14 for p in planes)]

        def body(i, carry):
            r, h = i // 2, pl.ds(pl.multiple_of((i % 2) * half, half), half)
            lv = {q: left(q, r, h).astype(F32) for q in lefts}
            rv = {q: right(q, r, h).astype(F32) for q in rights}
            for p in planes:
                total = acc[p, r, h, :]
                for q in lefts:
                    if 0 <= q - p < 14:
                        total = total + taps[0, q - p] * lv[q]
                for q in rights:
                    k = q + BEFORE + PLANES - p
                    if 0 <= k < 14:
                        total = total + taps[0, k] * rv[q]
                img[p, r, h, :] = total.astype(BF16)
            return carry

        lax.fori_loop(0, ROWS * 2, body, 0)

    def pair(j):
        done, count = sum(SIZES[:j]), SIZES[j]
        return pl.ds(PLANES - done - count + core * (2 * done + count - PLANES), count)

    def img_copy(k, j):
        to = peer(k)
        return remote(
            img.at[pair(j), share(to)], img_all.at[pair(j), :, slot(band), :],
            img_send.at[k, j], img_recv.at[k, j], to, space,
        )

    def rot_copy(k, j):
        to = peer(k)
        return remote(
            rot.at[pair(j), :, slot(to), :], out.at[pair(j), share(band)],
            rot_send.at[k, j], rot_recv.at[k, j], to, space,
        )

    def keep_copy(j):
        return pltpu.make_async_copy(rot.at[pair(j), :, slot(band), :], out.at[pair(j), share(band)], keep.at[j])

    def image(j):
        @pl.when(core == 0)
        def _():
            finish(
                range(PLANES - sum(SIZES[: j + 1]), PLANES - sum(SIZES[:j])),
                lambda q, r, h: far[BEFORE - 1 - q, r, h, :],
                lambda q, r, h: near[q, r, h, :],
            )

        @pl.when(core == 1)
        def _():
            finish(
                range(sum(SIZES[:j]), sum(SIZES[: j + 1])),
                lambda q, r, h: near[q, r, h, :],
                lambda q, r, h: far[q, r, h, :],
            )

        for k in SAME + CROSS:
            img_copy(k, j).start()
        img_all[pair(j), :, slot(band), :] = img[pair(j), share(band)]

    def spread(ref, j):
        v = ref[pair(j)]
        return jnp.concatenate([v[a, b] for a in range(SIZES[j]) for b in range(SHARE)], axis=1)

    def rotate(j):
        r = jnp.dot(all_panels[...], spread(img_all, j), preferred_element_type=F32).astype(BF16)
        parts = [r[:, i * LANES : (i + 1) * LANES] for i in range(SIZES[j] * SHARE)]
        rot[pair(j)] = jnp.stack(parts).reshape(SIZES[j], SHARE, ALL, LANES)

    def kinetic(j):
        r = lax.dot_general(
            spread(psi_all, j), spread(img_all, j), (((1,), (1,)), ((), ())), preferred_element_type=F32
        ).reshape(kacc.shape)
        kacc[...] = r if j == 0 else kacc[...] + r

    near_copy.wait_recv()
    arrived(0)
    image(0)
    relay(3)
    for k in (1, 3, 2):
        psi_copy(k, 1).start()
    relay(4)
    arrived(1)
    arrived(2)
    image(1)
    hear(0)
    tell(1)
    relay(5)
    relay(6)
    for k in (1, 3, 2):
        psi_copy(k, 2).start()
    arrived(3)
    arrived(4)
    image(2)
    relay(7)
    for k in (1, 3, 2):
        psi_copy(k, 3).start()
    psi_all[:, :, slot(partner), :] = psi_p[:, share(band)]
    arrived(5)
    image(3)
    arrived(6)
    image(4)
    hear(1)
    tell(2)
    for k in SAME + CROSS:
        panel_copy(k).start()

    for k in range(1, NY):
        for h in range(4):
            psi_copy(k, h).wait_recv()
    for j in range(CHUNKS):
        for k in range(1, BAND):
            img_copy(k, j).wait_recv()
        kinetic(j)

    def krs_copy(k):
        to, b, s = in_layer(k)
        return remote(ktwin.at[to], krs.at[k], krs_send.at[k], krs_recv.at[k], b, s)

    twin_copy = remote(kacc.at[:, 1 - core], ktwin, ktwin_send, ktwin_recv, band, twin)
    twin_copy.start()
    twin_copy.wait_recv()
    ktwin[...] += kacc[:, core]

    for k in sorted(range(1, layer), key=lambda k: -min(k, layer - k)):
        krs_copy(k).start()


    for k in range(1, BAND):
        panel_copy(k).wait_recv()

    def turn_out(j):
        rotate(j)
        for k in SAME + CROSS:
            rot_copy(k, j).start()
        keep_copy(j).start()

    turn_out(0)
    turn_out(1)
    krs[0] = ktwin[me]
    for k in range(1, layer):
        krs_copy(k).wait_recv()
    scale = 1.0 / (slabs * PLANES * ROWS * LANES)
    kpart[...] = jnp.sum(krs[...], axis=0) * scale

    def kz_copy(k):
        return remote(kpart, kz.at[z], kz_send.at[k], kz_recv.at[k], band, along(k))

    hear(2)
    far_first = sorted(range(1, nz), key=lambda k: -min(k, nz - k))
    for k in far_first:
        kz_copy(k).start()
    turn_out(2)
    turn_out(3)
    turn_out(4)
    kz[z] = kpart[...]
    for k in far_first:
        kz_copy(k).wait_recv()
    rows = pl.ds(pl.multiple_of(g * EIGHT, EIGHT), EIGHT)
    kin[rows, :] = jnp.sum(kz[...], axis=0)

    def ka_copy(k):
        return remote(
            kin.at[rows, :], kin.at[rows, :], ka_send.at[k], ka_recv.at[k], band, z * NG + lax.rem(g + k, NG)
        )

    for k in range(1, NG):
        ka_copy(k).start()
    for k in range(1, NG):
        ka_copy(k).wait_recv()
    for j in range(CHUNKS):
        for k in range(1, BAND):
            rot_copy(k, j).wait_recv()

    for j in range(CHUNKS):
        keep_copy(j).wait()
    for t in range(PLANES):
        part_copy(t).wait_send()
    @pl.when(inside)
    def _():
        for t in range(FACE):
            far_copy(t).wait_send()

    near_copy.wait_send()
    for k in range(1, NY):
        for h in range(4):
            psi_copy(k, h).wait_send()
    for k in range(1, BAND):
        panel_copy(k).wait_send()
        for j in range(CHUNKS):
            img_copy(k, j).wait_send()
            rot_copy(k, j).wait_send()

    def krs_sent(k, carry):
        krs_copy(k).wait_send()
        return carry

    twin_copy.wait_send()
    lax.fori_loop(1, layer, krs_sent, 0)
    for k in range(1, nz):
        kz_copy(k).wait_send()
    for k in range(1, NG):
        ka_copy(k).wait_send()


def on_device(nz, orbitals, filters, panels):
    vmem = pltpu.VMEM
    dma = pltpu.SemaphoreType.DMA
    slab = (PLANES, ROWS, ORB, LANES)
    mixed = (PLANES, SHARE, ALL, LANES)
    layer = BAND * 2
    rotated, kin = pl.pallas_call(
        functools.partial(kernel, nz),
        out_shape=(jax.ShapeDtypeStruct(slab, BF16), jax.ShapeDtypeStruct((ORB, ALL), F32)),
        in_specs=[
            pl.BlockSpec(memory_space=pltpu.SMEM),
            pl.BlockSpec(memory_space=pl.ANY),
            pl.BlockSpec(memory_space=pl.ANY),
        ],
        out_specs=(pl.BlockSpec(memory_space=pl.ANY), pl.BlockSpec(memory_space=vmem)),
        scratch_shapes=[
            vmem((ORB, PLANES, ROWS, LANES), BF16),
            vmem((ORB, ALL), BF16),
            vmem(slab, BF16),
            vmem(slab, BF16),
            vmem((FACE, ROWS, ORB, LANES), BF16),
            vmem((FACE, ROWS, ORB, LANES), BF16),
            vmem(slab, F32),
            vmem(slab, BF16),
            vmem(mixed, BF16),
            vmem(mixed, BF16),
            vmem(mixed, BF16),
            vmem((ALL, ALL), BF16),
            vmem((BAND * 2, 2, EIGHT, ALL), F32),
            vmem((BAND * 2, EIGHT, ALL), F32),
            vmem((layer, EIGHT, ALL), F32),
            vmem((nz, EIGHT, ALL), F32),
            vmem((EIGHT, ALL), F32),
            vmem((2 * LANES, LANES), BF16),
            dma((PLANES,)), dma((PLANES,)),
            dma((FACE,)), dma((FACE,)),
            dma, dma,
            dma((NY, 4)), dma((NY, 4)),
            dma((BAND,)), dma((BAND,)),
            dma((BAND, CHUNKS)), dma((BAND, CHUNKS)),
            dma((BAND, CHUNKS)), dma((BAND, CHUNKS)),
            dma, dma,
            dma((layer,)), dma((layer,)),
            dma((nz,)), dma((nz,)),
            dma((NG,)), dma((NG,)),
            pltpu.SemaphoreType.REGULAR((STEPS,)),
            dma((2,)),
            dma((CHUNKS,)),
        ],
        compiler_params=pltpu.CompilerParams(
            collective_id=0, has_side_effects=True, vmem_limit_bytes=57344 * 1024
        ),
    )(filters, orbitals, panels)
    return jnp.transpose(rotated, (2, 0, 1, 3)), kin


def solution(mesh):
    return jax.shard_map(
        functools.partial(on_device, mesh.shape["space"] // NG),
        mesh=mesh,
        in_specs=(P("band", "space", None, None), P(), P("band", None)),
        out_specs=(P("band", "space", None, None), P("band", None)),
        check_vma=False,
    )
```

```python
import functools

import jax
import jax.numpy as jnp
from jax import lax
from jax.experimental import pallas as pl
from jax.experimental.pallas import tpu as pltpu
from jax.sharding import PartitionSpec as P

MESH = pl.DeviceIdType.MESH
F32, BF16 = jnp.float32, jnp.bfloat16
BEFORE, AFTER = 7, 6
NY, NX = 4, 2
BAND = NY * NX
NG = 4
ORB, PLANES, ROWS, LANES = 32, 8, 16, 128
ALL = ORB * BAND
SIZES = (2, 2, 2, 1, 1)
CHUNKS = len(SIZES)
SHARE = ROWS // BAND
FACE = 7
EIGHT = ORB // NG
STEPS = 3
SAME, CROSS = (4, 2, 6), (3, 5, 1, 7)


def band_matrix(taps, row):
    a = lax.broadcasted_iota(jnp.int32, (LANES, LANES), 0)
    b = lax.broadcasted_iota(jnp.int32, (LANES, LANES), 1)
    total = jnp.zeros((LANES, LANES), F32)
    for k in range(14):
        total = jnp.where(a - b == k - BEFORE, taps[row, k], total)
    high = total.astype(BF16)
    low = (total - high.astype(F32)).astype(BF16)
    return jnp.concatenate([high, low], axis=0)


def kernel(
    nz,
    taps, orbitals_in, panels_in,
    out, kin,
    orbitals, panels, psi, psi_p, far, near, acc, img, psi_all, img_all, rot, all_panels, kacc, ktwin, krs, kz, kpart, zmat,
    part_send, part_recv, far_send, far_recv, near_send, near_recv, psi_send, psi_recv, pan_send, pan_recv,
    img_send, img_recv, rot_send, rot_recv, ktwin_send, ktwin_recv, krs_send, krs_recv, kz_send, kz_recv, ka_send, ka_recv, known, load, keep,
):
    band, space = lax.axis_index("band"), lax.axis_index("space")
    y, xl = band // NX, band % NX
    z, g, core = space // NG, space % NG, space % 2
    slabs = nz * NG
    partner = y * NX + (1 - xl)
    twin = space + 1 - 2 * core
    beyond = space - 1 + 2 * core
    inside = jnp.logical_and(beyond >= 0, beyond < slabs)
    layer = BAND * 2
    me = band * 2 + g // 2

    def remote(src, dst, send, recv, b, s):
        return pltpu.make_async_remote_copy(
            src_ref=src, dst_ref=dst, send_sem=send, recv_sem=recv, device_id=(b, s), device_id_type=MESH
        )

    def slot(b):
        return pl.ds(pl.multiple_of(b * ORB, ORB), ORB)

    def share(b):
        return pl.ds((b % NX) * (ROWS // NX) + (b // NX) * SHARE, SHARE)

    def peer(k):
        return lax.rem(band + k, BAND)

    loads = [
        pltpu.make_async_copy(orbitals_in, orbitals, load.at[0]),
        pltpu.make_async_copy(panels_in, panels, load.at[1]),
    ]
    for copy in loads:
        copy.start()

    barrier = pltpu.get_barrier_semaphore()

    def greet(b, s):
        pl.semaphore_signal(barrier, inc=1, device_id=(b, s), device_id_type=MESH)

    greet(partner, lax.rem(beyond + slabs, slabs))
    def along(k):
        return lax.rem(z + k + nz, nz) * NG + g

    for k in (1, -1):
        greet(band, along(k))

    def in_layer(k):
        to = lax.rem(me + k, layer)
        return to, to // 2, z * NG + (to % 2) * 2 + core

    def greet_layer(k, carry):
        _, b, s = in_layer(k)
        greet(b, s)
        return carry

    lax.fori_loop(1, layer, greet_layer, 0)
    greet(band, twin)
    greet(band, z * NG + lax.rem(g + 2, NG) + 1 - 2 * core)
    size = ROWS * ROWS
    a = lax.broadcasted_iota(jnp.int32, (size, size), 0)
    b = lax.broadcasted_iota(jnp.int32, (size, size), 1)
    swap = jnp.where((a // ROWS == b % ROWS) & (a % ROWS == b // ROWS), 1.0, 0.0).astype(BF16)

    def turn(p, carry):
        for h in range(ORB // ROWS):
            v = orbitals[h * ROWS : (h + 1) * ROWS, p].reshape(size, LANES)
            r = jnp.dot(swap, v, preferred_element_type=F32).astype(BF16)
            psi[p, :, h * ROWS : (h + 1) * ROWS, :] = r.reshape(ROWS, ROWS, LANES)
        return carry

    loads[0].wait()
    lax.fori_loop(0, PLANES, turn, 0)
    loads[1].wait()
    pl.semaphore_wait(barrier, 1 + 2 + 2 + layer - 1)

    def tell(step):
        for k in (1 << step, -(1 << step)):
            pl.semaphore_signal(known.at[step], inc=1, device_id=(band, along(k)), device_id_type=MESH)

    def hear(step):
        pl.semaphore_wait(known.at[step], 2)

    tell(0)

    def plane(t):
        return t + core * (PLANES - 1 - 2 * t)

    def part_copy(t):
        p = plane(t)
        if t < FACE:
            return remote(psi.at[p], psi_p.at[p], part_send.at[t], part_recv.at[t], partner, space)
        rows = pl.ds((1 - xl) * (ROWS // NX), ROWS // NX)
        return remote(psi.at[p, rows], psi_p.at[p, rows], part_send.at[t], part_recv.at[t], partner, space)

    def far_copy(t):
        return remote(psi_p.at[plane(t)], far.at[t], far_send.at[t], far_recv.at[t], partner, beyond)

    near_copy = remote(psi.at[pl.ds(1 - core, FACE)], near, near_send, near_recv, band, twin)

    for t in range(PLANES):
        part_copy(t).start()
    near_copy.start()

    def psi_copy(k, h):
        to = lax.rem(y + k, NY) * NX + xl
        src, owner = (psi, band) if h == 0 else (psi_p, partner)
        first, count = ((0, PLANES), (0, 4), (4, 2), (6, 2))[h]
        planes = pl.ds(first + core * (PLANES - count - 2 * first), count) if h else pl.ds(0, PLANES)
        return remote(
            src.at[planes, share(to)], psi_all.at[planes, :, slot(owner), :],
            psi_send.at[k, h], psi_recv.at[k, h], to, space,
        )

    def panel_copy(k):
        return remote(panels, all_panels.at[slot(band), :], pan_send.at[k], pan_recv.at[k], peer(k), space)

    for k in (1, 3, 2):
        psi_copy(k, 0).start()
    all_panels[slot(band), :] = panels[...]
    psi_all[:, :, slot(band), :] = psi[:, share(band)]

    @pl.when(jnp.logical_not(inside))
    def _():
        far[...] = jnp.zeros(far.shape, BF16)

    def relay(t):
        part_copy(t).wait_recv()
        if t < FACE:

            @pl.when(inside if t < AFTER else jnp.logical_and(inside, core == 1))
            def _():
                far_copy(t).start()

    def arrived(t):
        @pl.when(inside if t < AFTER else jnp.logical_and(inside, core == 0))
        def _():
            far_copy(t).wait_recv()

    zmat[...] = band_matrix(taps, 2)

    def along_z(p, carry):
        v = psi[p].reshape(ROWS * ORB, LANES)
        r = jnp.dot(jnp.concatenate([v, v], axis=1), zmat[...], preferred_element_type=F32)
        acc[p] = r.reshape(ROWS, ORB, LANES)
        return carry

    lax.fori_loop(0, PLANES, along_z, 0)
    relay(0)
    half = 16

    def along_y(i, carry):
        p, h = i // 2, pl.ds(pl.multiple_of((i % 2) * half, half), half)
        v = [psi[p, r, h, :].astype(F32) for r in range(ROWS)]
        for r in range(ROWS):
            total = acc[p, r, h, :]
            for k in range(14):
                if 0 <= r + k - BEFORE < ROWS:
                    total = total + taps[1, k] * v[r + k - BEFORE]
            acc[p, r, h, :] = total
        return carry

    lax.fori_loop(0, PLANES * 2, along_y, 0)
    relay(1)

    def along_x(i, carry):
        r, h = i // 2, pl.ds(pl.multiple_of((i % 2) * half, half), half)
        v = [psi[q, r, h, :].astype(F32) for q in range(PLANES)]
        for p in range(PLANES):
            total = acc[p, r, h, :]
            for k in range(14):
                if 0 <= p + k - BEFORE < PLANES:
                    total = total + taps[0, k] * v[p + k - BEFORE]
            acc[p, r, h, :] = total
        return carry

    lax.fori_loop(0, ROWS * 2, along_x, 0)
    relay(2)

    def finish(planes, left, right):
        lefts = [q for q in range(BEFORE) if any(0 <= q - p < 14 for p in planes)]
        rights = [q for q in range(AFTER) if any(0 <= q + BEFORE + PLANES - p < 14 for p in planes)]

        def body(i, carry):
            r, h = i // 2, pl.ds(pl.multiple_of((i % 2) * half, half), half)
            lv = {q: left(q, r, h).astype(F32) for q in lefts}
            rv = {q: right(q, r, h).astype(F32) for q in rights}
            for p in planes:
                total = acc[p, r, h, :]
                for q in lefts:
                    if 0 <= q - p < 14:
                        total = total + taps[0, q - p] * lv[q]
                for q in rights:
                    k = q + BEFORE + PLANES - p
                    if 0 <= k < 14:
                        total = total + taps[0, k] * rv[q]
                img[p, r, h, :] = total.astype(BF16)
            return carry

        lax.fori_loop(0, ROWS * 2, body, 0)

    def pair(j):
        done, count = sum(SIZES[:j]), SIZES[j]
        return pl.ds(PLANES - done - count + core * (2 * done + count - PLANES), count)

    def img_copy(k, j):
        to = peer(k)
        return remote(
            img.at[pair(j), share(to)], img_all.at[pair(j), :, slot(band), :],
            img_send.at[k, j], img_recv.at[k, j], to, space,
        )

    def rot_copy(k, j):
        to = peer(k)
        return remote(
            rot.at[pair(j), :, slot(to), :], out.at[pair(j), share(band)],
            rot_send.at[k, j], rot_recv.at[k, j], to, space,
        )

    def keep_copy(j):
        return pltpu.make_async_copy(rot.at[pair(j), :, slot(band), :], out.at[pair(j), share(band)], keep.at[j])

    def image(j):
        @pl.when(core == 0)
        def _():
            finish(
                range(PLANES - sum(SIZES[: j + 1]), PLANES - sum(SIZES[:j])),
                lambda q, r, h: far[BEFORE - 1 - q, r, h, :],
                lambda q, r, h: near[q, r, h, :],
            )

        @pl.when(core == 1)
        def _():
            finish(
                range(sum(SIZES[:j]), sum(SIZES[: j + 1])),
                lambda q, r, h: near[q, r, h, :],
                lambda q, r, h: far[q, r, h, :],
            )

        for k in SAME + CROSS:
            img_copy(k, j).start()
        img_all[pair(j), :, slot(band), :] = img[pair(j), share(band)]

    def spread(ref, j):
        v = ref[pair(j)]
        return jnp.concatenate([v[a, b] for a in range(SIZES[j]) for b in range(SHARE)], axis=1)

    def rotate(j):
        r = jnp.dot(all_panels[...], spread(img_all, j), preferred_element_type=F32).astype(BF16)
        parts = [r[:, i * LANES : (i + 1) * LANES] for i in range(SIZES[j] * SHARE)]
        rot[pair(j)] = jnp.stack(parts).reshape(SIZES[j], SHARE, ALL, LANES)

    def kinetic(j):
        r = lax.dot_general(
            spread(psi_all, j), spread(img_all, j), (((1,), (1,)), ((), ())), preferred_element_type=F32
        ).reshape(kacc.shape)
        kacc[...] = r if j == 0 else kacc[...] + r

    near_copy.wait_recv()
    arrived(0)
    image(0)
    relay(3)
    for k in (1, 3, 2):
        psi_copy(k, 1).start()
    relay(4)
    arrived(1)
    arrived(2)
    image(1)
    hear(0)
    tell(1)
    relay(5)
    relay(6)
    for k in (1, 3, 2):
        psi_copy(k, 2).start()
    arrived(3)
    arrived(4)
    image(2)
    relay(7)
    for k in (1, 3, 2):
        psi_copy(k, 3).start()
    psi_all[:, :, slot(partner), :] = psi_p[:, share(band)]
    arrived(5)
    image(3)
    arrived(6)
    image(4)
    hear(1)
    tell(2)
    for k in SAME + CROSS:
        panel_copy(k).start()

    for k in range(1, NY):
        for h in range(4):
            psi_copy(k, h).wait_recv()
    for j in range(CHUNKS):
        for k in range(1, BAND):
            img_copy(k, j).wait_recv()
        kinetic(j)

    def krs_copy(k):
        to, b, s = in_layer(k)
        return remote(ktwin.at[to], krs.at[k], krs_send.at[k], krs_recv.at[k], b, s)

    twin_copy = remote(kacc.at[:, 1 - core], ktwin, ktwin_send, ktwin_recv, band, twin)
    twin_copy.start()
    twin_copy.wait_recv()
    ktwin[...] += kacc[:, core]

    for k in sorted(range(1, layer), key=lambda k: -min(k, layer - k)):
        krs_copy(k).start()


    for k in range(1, BAND):
        panel_copy(k).wait_recv()

    def turn_out(j):
        rotate(j)
        for k in SAME + CROSS:
            rot_copy(k, j).start()
        keep_copy(j).start()

    turn_out(0)
    turn_out(1)
    krs[0] = ktwin[me]
    for k in range(1, layer):
        krs_copy(k).wait_recv()
    scale = 1.0 / (slabs * PLANES * ROWS * LANES)
    kpart[...] = jnp.sum(krs[...], axis=0) * scale

    def kz_copy(k):
        return remote(kpart, kz.at[z], kz_send.at[k], kz_recv.at[k], band, along(k))

    hear(2)
    far_first = sorted(range(1, nz), key=lambda k: -min(k, nz - k))
    for k in far_first:
        kz_copy(k).start()
    turn_out(2)
    turn_out(3)
    turn_out(4)
    kz[z] = kpart[...]
    for k in far_first:
        kz_copy(k).wait_recv()
    rows = pl.ds(pl.multiple_of(g * EIGHT, EIGHT), EIGHT)
    kin[rows, :] = jnp.sum(kz[...], axis=0)

    def ka_copy(k):
        return remote(
            kin.at[rows, :], kin.at[rows, :], ka_send.at[k], ka_recv.at[k], band, z * NG + lax.rem(g + k, NG)
        )

    for k in range(1, NG):
        ka_copy(k).start()
    for k in range(1, NG):
        ka_copy(k).wait_recv()
    for j in range(CHUNKS):
        for k in range(1, BAND):
            rot_copy(k, j).wait_recv()

    for j in range(CHUNKS):
        keep_copy(j).wait()
    for t in range(PLANES):
        part_copy(t).wait_send()
    @pl.when(inside)
    def _():
        for t in range(AFTER):
            far_copy(t).wait_send()

    @pl.when(jnp.logical_and(inside, core == 1))
    def _():
        far_copy(AFTER).wait_send()

    near_copy.wait_send()
    for k in range(1, NY):
        for h in range(4):
            psi_copy(k, h).wait_send()
    for k in range(1, BAND):
        panel_copy(k).wait_send()
        for j in range(CHUNKS):
            img_copy(k, j).wait_send()
            rot_copy(k, j).wait_send()

    def krs_sent(k, carry):
        krs_copy(k).wait_send()
        return carry

    twin_copy.wait_send()
    lax.fori_loop(1, layer, krs_sent, 0)
    for k in range(1, nz):
        kz_copy(k).wait_send()
    for k in range(1, NG):
        ka_copy(k).wait_send()


def on_device(nz, orbitals, filters, panels):
    vmem = pltpu.VMEM
    dma = pltpu.SemaphoreType.DMA
    slab = (PLANES, ROWS, ORB, LANES)
    mixed = (PLANES, SHARE, ALL, LANES)
    layer = BAND * 2
    rotated, kin = pl.pallas_call(
        functools.partial(kernel, nz),
        out_shape=(jax.ShapeDtypeStruct(slab, BF16), jax.ShapeDtypeStruct((ORB, ALL), F32)),
        in_specs=[
            pl.BlockSpec(memory_space=pltpu.SMEM),
            pl.BlockSpec(memory_space=pl.ANY),
            pl.BlockSpec(memory_space=pl.ANY),
        ],
        out_specs=(pl.BlockSpec(memory_space=pl.ANY), pl.BlockSpec(memory_space=vmem)),
        scratch_shapes=[
            vmem((ORB, PLANES, ROWS, LANES), BF16),
            vmem((ORB, ALL), BF16),
            vmem(slab, BF16),
            vmem(slab, BF16),
            vmem((FACE, ROWS, ORB, LANES), BF16),
            vmem((FACE, ROWS, ORB, LANES), BF16),
            vmem(slab, F32),
            vmem(slab, BF16),
            vmem(mixed, BF16),
            vmem(mixed, BF16),
            vmem(mixed, BF16),
            vmem((ALL, ALL), BF16),
            vmem((BAND * 2, 2, EIGHT, ALL), F32),
            vmem((BAND * 2, EIGHT, ALL), F32),
            vmem((layer, EIGHT, ALL), F32),
            vmem((nz, EIGHT, ALL), F32),
            vmem((EIGHT, ALL), F32),
            vmem((2 * LANES, LANES), BF16),
            dma((PLANES,)), dma((PLANES,)),
            dma((FACE,)), dma((FACE,)),
            dma, dma,
            dma((NY, 4)), dma((NY, 4)),
            dma((BAND,)), dma((BAND,)),
            dma((BAND, CHUNKS)), dma((BAND, CHUNKS)),
            dma((BAND, CHUNKS)), dma((BAND, CHUNKS)),
            dma, dma,
            dma((layer,)), dma((layer,)),
            dma((nz,)), dma((nz,)),
            dma((NG,)), dma((NG,)),
            pltpu.SemaphoreType.REGULAR((STEPS,)),
            dma((2,)),
            dma((CHUNKS,)),
        ],
        compiler_params=pltpu.CompilerParams(
            collective_id=0, has_side_effects=True, vmem_limit_bytes=57344 * 1024
        ),
    )(filters, orbitals, panels)
    return jnp.transpose(rotated, (2, 0, 1, 3)), kin


def solution(mesh):
    return jax.shard_map(
        functools.partial(on_device, mesh.shape["space"] // NG),
        mesh=mesh,
        in_specs=(P("band", "space", None, None), P(), P("band", None)),
        out_specs=(P("band", "space", None, None), P("band", None)),
        check_vma=False,
    )
```
